32 devices in a mesh: grp: 2 (over x), dev: 16 (over z, y, core).
Axes of the slice: x: 2, y: 2, z: 4, core: 2. Of those that a mesh axis runs over, the one named last changes fastest.
Arguments:
- kv_pool: bfloat16 [768, 64, 512], P(('grp', 'dev')), parts along dimension 0, may hold values from -6 to 6
- block_table: int32 [32, 24], P(('grp', 'dev')), parts along dimension 0, may hold values from 0 to 383, as said below
- lengths: int32 [32], P(('grp', 'dev')), parts along dimension 0, may hold values from 1 to 1536, as said below
- queries: bfloat16 [2, 32, 16384], P(None, ('grp', 'dev')), parts along dimension 1, may hold values from -32 to 32
- new_kv: bfloat16 [2, 32, 512], P(None, ('grp', 'dev')), parts along dimension 1, may hold values from -8 to 8
- residual_in: bfloat16 [2, 32, 7168], P(None, ('grp', 'dev')), parts along dimension 1, may hold values from -8 to 8
- norm_gain: bfloat16 [7168], replicated, may hold values from 0.099609375 to 1.8984375
- out_weight: bfloat16 [16384, 7168], P('dev'), may hold values from -0.375 to 0.375
- gate_weight: bfloat16 [7168, 9216], P(None, 'dev'), may hold values from -0.0625 to 0.0625
- up_weight: bfloat16 [7168, 9216], P(None, 'dev'), may hold values from -0.0625 to 0.0625
- down_weight: bfloat16 [9216, 7168], P('dev'), may hold values from -0.0625 to 0.0625
Outputs:
- layer_out: float32 [2, 32, 7168], P(None, ('grp', 'dev')), parts along dimension 1
The draws below stay inside these ranges and needn't reach their ends.
There are 2 independent parts, one for each index of `grp`. The reference program is written for one: setup_inputs(seed, part) draws one part's arguments, and reference() takes and returns one part's arrays. A program takes and returns all parts, laid end to end along the dimension named above; an argument that names none is the same for every part. Nothing has to cross between parts.
Inputs may be any that keep to these rules, and one draw needn't show every extreme that they name: `lengths`: one request of every serving group has exactly 1536 cached positions. `block_table`: request r is placed on device r: every entry of row r lies in that device's blocks, (r) * 24 to (r) * 24 + 23, and the requests of one device list each of its blocks exactly once.
All inputs are finite; a program needn't handle non-finite values.
Results may differ from the reference program's by a relative error of at most 0.0046.
Values may be sent and summed in bfloat16 or wider, within the bound.
A program may use at most 128 MiB of HBM per device.

```python
import jax
import jax.numpy as jnp
from jax import lax

D = 7168
HEADS = 64
HD = 256
FF = 9216
MAXB = 24
BLOCK = 64
STEPS = 2
BLK_DEV = 24
MAXLEN = 1536
REQS = 16
POOL = 384
N_DEV = 16


def shared_keys(key):
    normal_part = jax.random.normal(jax.random.fold_in(key, 1), (STEPS, REQS, 2 * HD), jnp.float32)
    return normal_part


def draw_lengths(key, part):
    key = jax.random.fold_in(key, 11)
    first_key, second_key, third_key = jax.random.split(key, 3)
    first_draw = jax.random.randint(first_key, (REQS,), 0, MAXLEN)
    second_draw = jax.random.randint(second_key, (REQS,), 0, MAXLEN)
    ragged = 1 + first_draw * second_draw // MAXLEN
    longest = jax.random.randint(third_key, (), 0, REQS)
    return jnp.where(jnp.arange(REQS) == longest, MAXLEN, ragged).astype(jnp.int32)


def draw_block_table(key, part):
    key = jax.random.fold_in(key, 12)
    device_keys = jax.random.split(key, N_DEV)
    orders = jax.vmap(lambda device_key: jax.random.permutation(device_key, BLK_DEV))(device_keys)
    offsets = (jnp.arange(N_DEV, dtype=jnp.int32) * BLK_DEV)[:, None]
    return (orders.astype(jnp.int32) + offsets).reshape(REQS, MAXB)


def draw_new_kv(key, part):
    normal_part = shared_keys(key)
    return jnp.clip(normal_part, -6.0, 6.0).astype(jnp.bfloat16)


def draw_queries(key, part):
    key = jax.random.fold_in(key, 22)
    return jnp.clip(jax.random.normal(key, (STEPS, REQS, HEADS * HD), jnp.float32), -6.0, 6.0).astype(jnp.bfloat16)


def draw_residual_in(key, part):
    key = jax.random.fold_in(key, 23)
    row_key, column_key, noise_key = jax.random.split(key, 3)
    row_scale = jnp.exp(jax.random.uniform(row_key, (STEPS, REQS, 1), jnp.float32, jnp.log(0.1), 0.0))
    column_scale = jnp.exp(jax.random.uniform(column_key, (D,), jnp.float32, jnp.log(0.1), 0.0))
    noise = jnp.clip(jax.random.normal(noise_key, (STEPS, REQS, D), jnp.float32), -4.0, 4.0)
    return (noise * row_scale * column_scale).astype(jnp.bfloat16)


def block_levels(key, extent, pieces, smallest, high):
    def one(dim, parts):
        heights = jax.random.uniform(jax.random.fold_in(jax.random.fold_in(key, 6), dim), (parts,), jnp.float32, smallest / len(pieces), high / len(pieces))
        return jnp.repeat(jnp.exp(heights), extent[dim] // parts).reshape((-1,) + (1,) * (len(extent) - dim - 1))

    level = one(*pieces[0])
    for cut in pieces[1:]:
        level = level * one(*cut)
    return level


def bell_draw(own_key, shape, deviation, reach, shards=(), kind=jnp.bfloat16):
    drawn = jax.random.normal(own_key, shape, jnp.float32) * deviation
    if len(shards) > 0:
        drawn = block_levels(own_key, shape, shards, -0.22, 0.18) * drawn
    return jnp.clip(drawn, min=-reach, max=reach).astype(kind)


def setup_inputs(seed: int = 0, part: int = 0) -> dict:
    key_of = jax.random.split(jax.random.key(seed), 12)
    part_splits = jax.random.split(jax.random.fold_in(key_of[11], part), 12)
    return {
        "kv_pool": bell_draw(part_splits[0], (POOL, BLOCK, 2 * HD), 1.0, 6.0, ((0, 16),)),
        "block_table": draw_block_table(jax.random.fold_in(jax.random.fold_in(key_of[11], part), 71), part),
        "lengths": draw_lengths(jax.random.fold_in(jax.random.fold_in(key_of[11], part), 71), part),
        "queries": draw_queries(jax.random.fold_in(jax.random.fold_in(key_of[11], part), 71), part),
        "new_kv": draw_new_kv(jax.random.fold_in(jax.random.fold_in(key_of[11], part), 71), part),
        "residual_in": draw_residual_in(jax.random.fold_in(jax.random.fold_in(key_of[11], part), 71), part),
        "norm_gain": jnp.clip(1.0 + 0.18 * jax.random.normal(key_of[6], (D,), jnp.float32), 0.099609375, 1.8984375).astype(jnp.bfloat16),
        "out_weight": bell_draw(key_of[7], (HEADS * HD, D), HD ** -0.5, 0.375, ((0, 16),)),
        "gate_weight": bell_draw(key_of[8], (D, FF), D ** -0.5, 0.0625, ((1, 16),)),
        "up_weight": bell_draw(key_of[9], (D, FF), D ** -0.5, 0.0625, ((1, 16),)),
        "down_weight": bell_draw(key_of[10], (FF, D), FF ** -0.5, 0.0625, ((0, 16),)),
    }


def attend_one(query_row, cache_rows, fresh_rows, length_value, step_index):
    scale_factor = HD ** (-0.5)
    query_heads = query_row.reshape(HEADS, HD)
    all_rows = jnp.concatenate([cache_rows, fresh_rows], axis=0)
    scores = jnp.dot(query_heads.astype(jnp.float32), all_rows[:, :HD].astype(jnp.float32).T) * scale_factor
    positions = jnp.arange(MAXLEN + STEPS, dtype=jnp.int32)
    visible = jnp.where(positions < MAXLEN, positions < length_value, positions - MAXLEN <= step_index)
    scores = jnp.where(visible[None, :], scores, -jnp.inf)
    largest = lax.optimization_barrier(jnp.max(scores, axis=-1, keepdims=True))
    weights = jnp.exp(scores - largest)
    probs = (weights / lax.optimization_barrier(jnp.sum(weights, axis=-1, keepdims=True))).astype(jnp.bfloat16)
    attended = jnp.dot(probs, all_rows[:, HD:], preferred_element_type=jnp.float32)
    return attended.astype(jnp.bfloat16).reshape(HEADS * HD)

def reference(kv_pool, block_table, lengths, queries, new_kv, residual_in, norm_gain, out_weight, gate_weight, up_weight, down_weight):
    fresh_all = jnp.transpose(new_kv, (1, 0, 2))
    outputs = []
    for step_index in range(STEPS):

        def one_request(packed, step_index=step_index):
            query_row, table_row, length_value, fresh_rows = packed
            cache_rows = kv_pool[table_row].reshape(MAXLEN, 2 * HD)
            return attend_one(query_row, cache_rows, fresh_rows, length_value, step_index)
        attended = lax.map(one_request, (queries[step_index], block_table, lengths, fresh_all))
        projected = jnp.dot(attended, out_weight, preferred_element_type=jnp.float32)
        state = residual_in[step_index].astype(jnp.float32) + projected
        scale_rows = lax.rsqrt(lax.optimization_barrier(jnp.mean(state * state, axis=-1, keepdims=True)) + 1e-06)
        normed = (state * scale_rows * norm_gain.astype(jnp.float32)).astype(jnp.bfloat16)
        gate_out = jnp.dot(normed, gate_weight, preferred_element_type=jnp.float32)
        up_out = jnp.dot(normed, up_weight, preferred_element_type=jnp.float32)
        hidden_units = (jax.nn.silu(gate_out) * up_out).astype(jnp.bfloat16)
        outputs.append(state + jnp.dot(hidden_units, down_weight, preferred_element_type=jnp.float32))
    return jnp.stack(outputs)
```

```python
import functools

import jax
import jax.numpy as jnp
from jax import lax
from jax.experimental import pallas as pl
from jax.experimental.pallas import tpu as pltpu
from jax.sharding import PartitionSpec as P

F32 = jnp.float32
BF16 = jnp.bfloat16
MESH = pl.DeviceIdType.MESH
WIDE = 1024


def layer_kernel(
    n,
    table_ref,
    length_ref,
    q_ref,
    fresh_ref,
    res_ref,
    gain_ref,
    kv_hbm,
    wo_hbm,
    wg_hbm,
    wu_hbm,
    wd_hbm,
    out_ref,
    kv,
    wo,
    wg,
    wu,
    wd,
    att,
    att_send,
    att_recv,
    att_wide,
    lhs,
    part,
    send1,
    recv1,
    acc1,
    send2,
    recv2,
    acc2,
    send3,
    recv3,
    state,
    rows_all,
    rows_wide,
    normed,
    kv_sem,
    w_sem,
    att_ssem,
    att_rsem,
    s1_sem,
    r1_sem,
    s2_sem,
    r2_sem,
    s3_sem,
    r3_sem,
    gz_ssem,
    gz_rsem,
    gy_ssem,
    gy_rsem,
    gc_ssem,
    gc_rsem,
):
    me = lax.axis_index("dev")
    nz = n // 4
    core, y, z = lax.rem(me, 2), lax.rem(me // 2, 2), me // 4
    chunks = state.shape[0]
    heads_dev = lhs.shape[1] // 256
    rows = 2 * n
    width = chunks * WIDE

    def slot_of(i):
        return lax.rem(i, 2) * (n // 2) + lax.rem(i // 2, 2) * nz + i // 4

    my_slot = slot_of(me)
    twin = me + 1 - 2 * core
    y_peer = me + 2 - 4 * y

    def z_peer(off):
        other = lax.rem(z + off, nz)
        return other, other * 4 + y * 2 + core

    kv_copy = pltpu.make_async_copy(kv_hbm, kv, kv_sem)
    kv_copy.start()

    def columns(c):
        return pl.ds(c * WIDE, WIDE)

    wo_copies = [
        pltpu.make_async_copy(wo_hbm.at[:, columns(c)], wo.at[:, columns(c)], w_sem.at[0, c])
        for c in range(chunks)
    ]
    wg_copies = [
        pltpu.make_async_copy(wg_hbm.at[columns(c)], wg.at[columns(c)], w_sem.at[1, c])
        for c in range(chunks)
    ]
    wu_copies = [
        pltpu.make_async_copy(wu_hbm.at[columns(c)], wu.at[columns(c)], w_sem.at[2, c])
        for c in range(chunks)
    ]
    wd_copies = [
        pltpu.make_async_copy(wd_hbm.at[:, columns(c)], wd.at[:, columns(c)], w_sem.at[3, c])
        for c in range(chunks)
    ]
    for copy in wo_copies:
        copy.start()
    for pair in zip(wg_copies, wu_copies):
        for copy in pair:
            copy.start()
    for copy in wd_copies:
        copy.start()

    barrier = pltpu.get_barrier_semaphore()

    def greet(off, carry):
        pl.semaphore_signal(
            barrier, inc=1, device_id={"dev": lax.rem(me + off, n)}, device_id_type=MESH
        )
        return carry

    lax.fori_loop(1, n, greet, 0)

    positions = kv.shape[0]
    blocks = table_ref.shape[1]
    block_rows = positions // blocks
    place = lax.broadcasted_iota(jnp.int32, (1, positions), 1)
    block_of = place // block_rows
    order = jnp.zeros((1, positions), jnp.int32)
    for j in range(blocks):
        order = jnp.where(block_of == lax.rem(table_ref[0, j], blocks), j, order)
    position = order * block_rows + (place - block_of * block_rows)
    visible = position < length_ref[0]

    q = q_ref[...]
    q_rows = q.shape[0]
    contract_last = (((1,), (1,)), ((), ()))
    fresh = fresh_ref[...]
    fresh_scores = (
        lax.dot_general(q, fresh[:, :256], contract_last, preferred_element_type=F32) * 0.0625
    )
    step_of_row = lax.rem(lax.broadcasted_iota(jnp.int32, (q_rows, 16), 0), 2)
    fresh_step = lax.broadcasted_iota(jnp.int32, (q_rows, 16), 1)
    fresh_scores = jnp.where(fresh_step <= step_of_row, fresh_scores, -jnp.inf)
    kv_copy.wait()
    scores = (
        lax.dot_general(q, kv[:, :256], contract_last, preferred_element_type=F32) * 0.0625
    )
    scores = jnp.where(visible, scores, -jnp.inf)
    largest = jnp.maximum(
        jnp.max(scores, axis=1, keepdims=True), jnp.max(fresh_scores, axis=1, keepdims=True)
    )
    weights = jnp.exp(scores - largest)
    fresh_weights = jnp.exp(fresh_scores - largest)
    total = jnp.sum(weights, axis=1, keepdims=True) + jnp.sum(
        fresh_weights, axis=1, keepdims=True
    )
    probs = (weights / total).astype(BF16)
    fresh_probs = (fresh_weights / total).astype(BF16)
    attended = jnp.dot(probs, kv[:, 256:], preferred_element_type=F32) + jnp.dot(
        fresh_probs, fresh[:, 256:], preferred_element_type=F32
    )
    if heads_dev < 4:
        att[...] = jnp.zeros_like(att)
    for h in range(heads_dev):
        for half in range(2):
            att[pl.ds(h * 2 + half, rows, stride=8), :] = attended[
                h * rows : (h + 1) * rows, half * 128 : (half + 1) * 128
            ]
    att_send[...] = att[...].astype(BF16).reshape(att_send.shape)

    pl.semaphore_wait(barrier, n - 1)

    def att_copy(off):
        peer = lax.rem(me + off, n)
        return pltpu.make_async_remote_copy(
            src_ref=att_send.at[peer],
            dst_ref=att_recv.at[my_slot],
            send_sem=att_ssem.at[off],
            recv_sem=att_rsem.at[my_slot],
            device_id={"dev": peer},
            device_id_type=MESH,
        )

    def start_att(off, carry):
        att_copy(off).start()
        return carry

    lax.fori_loop(1, n, start_att, 0)
    att_recv[my_slot] = att_send[me]

    def wait_att(off, carry):
        source = slot_of(lax.rem(me + off, n))
        pltpu.make_async_remote_copy(
            src_ref=att_send.at[0],
            dst_ref=att_recv.at[source],
            send_sem=att_ssem.at[off],
            recv_sem=att_rsem.at[source],
            device_id={"dev": twin},
            device_id_type=MESH,
        ).wait_recv()
        return carry

    lax.fori_loop(1, n, wait_att, 0)
    att_wide[...] = att_recv[...].astype(F32).reshape(att_wide.shape)
    for k in range(2 * heads_dev):
        lhs[:, k * 128 : (k + 1) * 128] = att_wide[pl.ds(k, rows, stride=8), :].astype(BF16)

    half_rows, quarter_rows = n * 8, n * 4
    group = (chunks + 6) // 7

    def move(src, dst, ssem, rsem, peer):
        return pltpu.make_async_remote_copy(
            src_ref=src,
            dst_ref=dst,
            send_sem=ssem,
            recv_sem=rsem,
            device_id={"dev": peer},
            device_id_type=MESH,
        )

    def reduce_rows(turn, product):
        def to_twin(c):
            return move(
                send1.at[turn, c], recv1.at[turn, c], s1_sem.at[turn, c], r1_sem.at[turn, c], twin
            )

        def to_y(c):
            return move(
                send2.at[turn, c], recv2.at[turn, c], s2_sem.at[turn, c], r2_sem.at[turn, c], y_peer
            )

        def to_z(c, off):
            other, peer = z_peer(off)
            return move(
                send3.at[turn, c, other],
                recv3.at[turn, c, off],
                s3_sem.at[turn, c, off],
                r3_sem.at[turn, c, off],
                peer,
            )

        def first(c):
            tile = product(c)
            for j in range(8):
                part[c, pl.ds(j, rows, stride=8), :] = tile[:, j * 128 : (j + 1) * 128]
            away = pl.multiple_of((1 - core) * half_rows, half_rows)
            send1[turn, c] = part[c, pl.ds(away, half_rows), :].astype(BF16)
            to_twin(c).start()

        def second(c):
            to_twin(c).wait_recv()
            home = pl.multiple_of(core * half_rows, half_rows)
            acc1[c] = part[c, pl.ds(home, half_rows), :] + recv1[turn, c].astype(F32)
            away = pl.multiple_of((1 - y) * quarter_rows, quarter_rows)
            send2[turn, c] = acc1[c, pl.ds(away, quarter_rows), :].astype(BF16)
            to_y(c).start()

        def third(c):
            to_y(c).wait_recv()
            home = pl.multiple_of(y * quarter_rows, quarter_rows)
            held = acc1[c, pl.ds(home, quarter_rows), :] + recv2[turn, c].astype(F32)
            held = held.reshape(nz, 16, 128)
            acc2[c] = held
            send3[turn, c] = held.astype(BF16)
            for off in range(1, nz):
                to_z(c, off).start()

        for step in range(chunks + 2):
            if step < chunks:
                first(step)
            if 0 <= step - 1 < chunks:
                second(step - 1)
            if 0 <= step - 2 < chunks:
                third(step - 2)
        sums = []
        for c in range(chunks):
            total = acc2[c, z]
            for off in range(1, nz):
                to_z(c, off).wait_recv()
                total = total + recv3[turn, c, off].astype(F32)
            sums.append(total)

        def finish():
            for c in range(chunks):
                to_twin(c).wait_send()
                to_y(c).wait_send()
                for off in range(1, nz):
                    to_z(c, off).wait_send()

        return sums, finish

    def project(c):
        wo_copies[c].wait()
        return jnp.dot(lhs[...], wo[:, columns(c)], preferred_element_type=F32)

    sums, finish_first = reduce_rows(0, project)
    square = jnp.zeros((16, 128), F32)
    for c in range(chunks):
        row = res_ref[c].astype(F32) + sums[c]
        state[c] = row
        square = square + row * row
    scale0 = lax.rsqrt(jnp.sum(square[:8], keepdims=True) / width + 1e-06)
    scale1 = lax.rsqrt(jnp.sum(square[8:], keepdims=True) / width + 1e-06)
    scale = jnp.concatenate(
        [jnp.broadcast_to(scale0, (8, 128)), jnp.broadcast_to(scale1, (8, 128))], axis=0
    )

    my_rows = pl.multiple_of(my_slot * 16, 16)
    y_rows = pl.multiple_of((core * 2 + y) * quarter_rows, quarter_rows)
    core_rows = pl.multiple_of(core * half_rows, half_rows)
    y_in_rows = pl.multiple_of((core * 2 + 1 - y) * quarter_rows, quarter_rows)
    core_in_rows = pl.multiple_of((1 - core) * half_rows, half_rows)

    def spread_z(c, off):
        block = rows_all.at[c, pl.ds(my_rows, 16)]
        return move(block, block, gz_ssem.at[c, off], gz_rsem.at[c, off], z_peer(off)[1])

    def landed_z(c, off):
        source = lax.rem(z + nz - off, nz)
        block = rows_all.at[c, pl.ds(pl.multiple_of(y_rows + source * 16, 16), 16)]
        return move(block, block, gz_ssem.at[c, off], gz_rsem.at[c, off], z_peer(off)[1])

    def spread_y(c, start):
        block = rows_all.at[c, pl.ds(start, quarter_rows)]
        return move(block, block, gy_ssem.at[c], gy_rsem.at[c], y_peer)

    def spread_core(c, start):
        block = rows_all.at[c, pl.ds(start, half_rows)]
        return move(block, block, gc_ssem.at[c], gc_rsem.at[c], twin)

    for c in range(chunks):
        gain = gain_ref[c].astype(F32)
        gain = jnp.concatenate([gain, gain], axis=0)
        rows_all[c, pl.ds(my_rows, 16), :] = (state[c] * scale * gain).astype(BF16)
        for off in range(1, nz):
            spread_z(c, off).start()

    gate = jnp.zeros((rows, wg.shape[1]), F32)
    up = jnp.zeros((rows, wg.shape[1]), F32)
    for step in range(chunks + 2):
        if step < chunks:
            for off in range(1, nz):
                landed_z(step, off).wait_recv()
            spread_y(step, y_rows).start()
        if 0 <= step - 1 < chunks:
            c = step - 1
            spread_y(c, y_in_rows).wait_recv()
            spread_core(c, core_rows).start()
        if 0 <= step - 2 < chunks:
            c = step - 2
            spread_core(c, core_in_rows).wait_recv()
            rows_wide[...] = rows_all[c].astype(F32)
            for j in range(8):
                normed[:, j * 128 : (j + 1) * 128] = rows_wide[
                    pl.ds(j, rows, stride=8), :
                ].astype(BF16)
            held = normed[...]
            wg_copies[c].wait()
            wu_copies[c].wait()
            gate = gate + jnp.dot(held, wg[columns(c), :], preferred_element_type=F32)
            up = up + jnp.dot(held, wu[columns(c), :], preferred_element_type=F32)

    hidden = (gate / (1.0 + jnp.exp(-gate)) * up).astype(BF16)

    def down(c):
        wd_copies[c].wait()
        return jnp.dot(hidden, wd[:, columns(c)], preferred_element_type=F32)

    sums, finish_second = reduce_rows(1, down)
    for c in range(chunks):
        out_ref[c] = state[c] + sums[c]

    def drain_att(off, carry):
        att_copy(off).wait_send()
        return carry

    lax.fori_loop(1, n, drain_att, 0)
    finish_first()
    finish_second()
    for c in range(chunks):
        for off in range(1, nz):
            spread_z(c, off).wait_send()
        spread_y(c, y_rows).wait_send()
        spread_core(c, core_rows).wait_send()


def per_device(
    n,
    kv_pool,
    block_table,
    lengths,
    queries,
    new_kv,
    residual_in,
    norm_gain,
    out_weight,
    gate_weight,
    up_weight,
    down_weight,
):
    steps = queries.shape[0]
    head_width = new_kv.shape[2] // 2
    head_count = queries.shape[2] // head_width
    heads_dev = head_count // n
    width = residual_in.shape[2]
    chunks = width // WIDE
    units = gate_weight.shape[1]
    nz = n // 4
    positions = kv_pool.shape[0] * kv_pool.shape[1]

    q = (
        queries.reshape(steps, n, heads_dev, head_width)
        .transpose(2, 1, 0, 3)
        .reshape(head_count * steps, head_width)
    )
    fresh = jnp.pad(new_kv.reshape(steps, -1), ((0, 16 - steps), (0, 0)))
    residual = (
        residual_in.reshape(steps, chunks, 8, 128)
        .transpose(1, 0, 2, 3)
        .reshape(chunks, 8 * steps, 128)
    )
    gain = norm_gain.reshape(chunks, 8, 128)
    cache = kv_pool.reshape(positions, 2 * head_width)

    vmem = pl.BlockSpec(memory_space=pltpu.VMEM)
    smem = pl.BlockSpec(memory_space=pltpu.SMEM)
    hbm = pl.BlockSpec(memory_space=pl.ANY)
    dma = pltpu.SemaphoreType.DMA
    out = pl.pallas_call(
        functools.partial(layer_kernel, n),
        out_shape=jax.ShapeDtypeStruct((chunks, 16, 128), F32),
        in_specs=[smem, smem, vmem, vmem, vmem, vmem] + [hbm] * 5,
        out_specs=vmem,
        scratch_shapes=[
            pltpu.VMEM((positions, 2 * head_width), BF16),
            pltpu.VMEM(out_weight.shape, BF16),
            pltpu.VMEM(gate_weight.shape, BF16),
            pltpu.VMEM(up_weight.shape, BF16),
            pltpu.VMEM(down_weight.shape, BF16),
            pltpu.VMEM((n * 16, 128), F32),
            pltpu.VMEM((n, 16, 128), BF16),
            pltpu.VMEM((n, 16, 128), BF16),
            pltpu.VMEM((n * 16, 128), F32),
            pltpu.VMEM((2 * n, heads_dev * head_width), BF16),
            pltpu.VMEM((chunks, n * 16, 128), F32),
            pltpu.VMEM((2, chunks, n * 8, 128), BF16),
            pltpu.VMEM((2, chunks, n * 8, 128), BF16),
            pltpu.VMEM((chunks, n * 8, 128), F32),
            pltpu.VMEM((2, chunks, n * 4, 128), BF16),
            pltpu.VMEM((2, chunks, n * 4, 128), BF16),
            pltpu.VMEM((chunks, nz, 16, 128), F32),
            pltpu.VMEM((2, chunks, nz, 16, 128), BF16),
            pltpu.VMEM((2, chunks, nz, 16, 128), BF16),
            pltpu.VMEM((chunks, 16, 128), F32),
            pltpu.VMEM((chunks, n * 16, 128), BF16),
            pltpu.VMEM((n * 16, 128), F32),
            pltpu.VMEM((2 * n, WIDE), BF16),
            dma(()),
            dma((4, chunks)),
            dma((n,)),
            dma((n,)),
            dma((2, chunks)),
            dma((2, chunks)),
            dma((2, chunks)),
            dma((2, chunks)),
            dma((2, chunks, nz)),
            dma((2, chunks, nz)),
            dma((chunks, nz)),
            dma((chunks, nz)),
            dma((chunks,)),
            dma((chunks,)),
            dma((chunks,)),
            dma((chunks,)),
        ],
        compiler_params=pltpu.CompilerParams(
            collective_id=0, has_side_effects=True, vmem_limit_bytes=60 * 1024 * 1024
        ),
        cost_estimate=pl.CostEstimate(
            flops=2 * 2 * n * (out_weight.size + 3 * gate_weight.size),
            bytes_accessed=2 * (out_weight.size + 3 * gate_weight.size + cache.size),
            transcendentals=0,
        ),
        name="decode_layer",
    )(
        block_table,
        lengths,
        q,
        fresh,
        residual,
        gain,
        cache,
        out_weight,
        gate_weight,
        up_weight,
        down_weight,
    )
    return (
        out.reshape(chunks, steps, 8, 128).transpose(1, 0, 2, 3).reshape(steps, 1, width)
    )


def solution(mesh):
    placed = (
        P(("grp", "dev"), None, None),
        P(("grp", "dev"), None),
        P(("grp", "dev")),
        P(None, ("grp", "dev"), None),
        P(None, ("grp", "dev"), None),
        P(None, ("grp", "dev"), None),
        P(),
        P("dev", None),
        P(None, "dev"),
        P(None, "dev"),
        P("dev", None),
    )
    return jax.shard_map(
        functools.partial(per_device, mesh.shape["dev"]),
        mesh=mesh,
        in_specs=placed,
        out_specs=P(None, ("grp", "dev"), None),
        check_vma=False,
    )
```

```python
import functools

import jax
import jax.numpy as jnp
from jax import lax
from jax.experimental import pallas as pl
from jax.experimental.pallas import tpu as pltpu
from jax.sharding import PartitionSpec as P

F32 = jnp.float32
BF16 = jnp.bfloat16
MESH = pl.DeviceIdType.MESH
RS_GROUPS = 2
AG_GROUPS = 2
WIDE = 1024


def layer_kernel(
    n,
    table_ref,
    length_ref,
    q_ref,
    fresh_ref,
    res_ref,
    gain_ref,
    kv_hbm,
    wo_hbm,
    wg_hbm,
    wu_hbm,
    wd_hbm,
    out_ref,
    kv,
    wo,
    wg,
    wu,
    wd,
    att,
    att_send,
    att_recv,
    att_wide,
    lhs,
    part,
    send1,
    recv1,
    acc1,
    send2,
    recv2,
    acc2,
    send3,
    recv3,
    state,
    rows_all,
    rows_wide,
    normed,
    kv_sem,
    w_sem,
    att_ssem,
    att_rsem,
    s1_sem,
    r1_sem,
    s2_sem,
    r2_sem,
    s3_sem,
    r3_sem,
    gz_ssem,
    gz_rsem,
    gy_ssem,
    gy_rsem,
    gc_ssem,
    gc_rsem,
):
    me = lax.axis_index("dev")
    nz = n // 4
    core, y, z = lax.rem(me, 2), lax.rem(me // 2, 2), me // 4
    chunks = state.shape[0]
    heads_dev = lhs.shape[1] // 256
    rows = 2 * n
    width = chunks * WIDE

    def slot_of(i):
        return lax.rem(i, 2) * (n // 2) + lax.rem(i // 2, 2) * nz + i // 4

    my_slot = slot_of(me)
    twin = me + 1 - 2 * core
    y_peer = me + 2 - 4 * y

    def z_peer(off):
        other = lax.rem(z + off, nz)
        return other, other * 4 + y * 2 + core

    kv_copy = pltpu.make_async_copy(kv_hbm, kv, kv_sem)
    kv_copy.start()

    def columns(c):
        return pl.ds(c * WIDE, WIDE)

    wo_copies = [
        pltpu.make_async_copy(wo_hbm.at[:, columns(c)], wo.at[:, columns(c)], w_sem.at[0, c])
        for c in range(chunks)
    ]
    wg_copies = [
        pltpu.make_async_copy(wg_hbm.at[:, columns(c)], wg.at[:, columns(c)], w_sem.at[1, c])
        for c in range(chunks)
    ]
    wu_copies = [
        pltpu.make_async_copy(wu_hbm.at[:, columns(c)], wu.at[:, columns(c)], w_sem.at[2, c])
        for c in range(chunks)
    ]
    wd_copies = [
        pltpu.make_async_copy(wd_hbm.at[:, columns(c)], wd.at[:, columns(c)], w_sem.at[3, c])
        for c in range(chunks)
    ]
    for copy in wo_copies:
        copy.start()
    for pair in zip(wg_copies, wu_copies):
        for copy in pair:
            copy.start()
    for copy in wd_copies:
        copy.start()

    barrier = pltpu.get_barrier_semaphore()

    def greet(off, carry):
        pl.semaphore_signal(
            barrier, inc=1, device_id={"dev": lax.rem(me + off, n)}, device_id_type=MESH
        )
        return carry

    lax.fori_loop(1, n, greet, 0)

    positions = kv.shape[0]
    blocks = table_ref.shape[1]
    block_rows = positions // blocks
    place = lax.broadcasted_iota(jnp.int32, (1, positions), 1)
    block_of = place // block_rows
    order = jnp.zeros((1, positions), jnp.int32)
    for j in range(blocks):
        order = jnp.where(block_of == lax.rem(table_ref[0, j], blocks), j, order)
    position = order * block_rows + (place - block_of * block_rows)
    visible = position < length_ref[0]

    q = q_ref[...]
    q_rows = q.shape[0]
    contract_last = (((1,), (1,)), ((), ()))
    fresh = fresh_ref[...]
    fresh_scores = (
        lax.dot_general(q, fresh[:, :256], contract_last, preferred_element_type=F32) * 0.0625
    )
    step_of_row = lax.rem(lax.broadcasted_iota(jnp.int32, (q_rows, 16), 0), 2)
    fresh_step = lax.broadcasted_iota(jnp.int32, (q_rows, 16), 1)
    fresh_scores = jnp.where(fresh_step <= step_of_row, fresh_scores, -jnp.inf)
    kv_copy.wait()
    scores = (
        lax.dot_general(q, kv[:, :256], contract_last, preferred_element_type=F32) * 0.0625
    )
    scores = jnp.where(visible, scores, -jnp.inf)
    largest = jnp.maximum(
        jnp.max(scores, axis=1, keepdims=True), jnp.max(fresh_scores, axis=1, keepdims=True)
    )
    weights = jnp.exp(scores - largest)
    fresh_weights = jnp.exp(fresh_scores - largest)
    total = jnp.sum(weights, axis=1, keepdims=True) + jnp.sum(
        fresh_weights, axis=1, keepdims=True
    )
    probs = (weights / total).astype(BF16)
    fresh_probs = (fresh_weights / total).astype(BF16)
    attended = jnp.dot(probs, kv[:, 256:], preferred_element_type=F32) + jnp.dot(
        fresh_probs, fresh[:, 256:], preferred_element_type=F32
    )
    if heads_dev < 4:
        att[...] = jnp.zeros_like(att)
    for h in range(heads_dev):
        for half in range(2):
            att[pl.ds(h * 2 + half, rows, stride=8), :] = attended[
                h * rows : (h + 1) * rows, half * 128 : (half + 1) * 128
            ]
    att_send[...] = att[...].astype(BF16).reshape(att_send.shape)

    pl.semaphore_wait(barrier, n - 1)

    def att_copy(off):
        peer = lax.rem(me + off, n)
        return pltpu.make_async_remote_copy(
            src_ref=att_send.at[peer],
            dst_ref=att_recv.at[my_slot],
            send_sem=att_ssem.at[off],
            recv_sem=att_rsem.at[my_slot],
            device_id={"dev": peer},
            device_id_type=MESH,
        )

    def start_att(off, carry):
        att_copy(off).start()
        return carry

    lax.fori_loop(1, n, start_att, 0)
    att_recv[my_slot] = att_send[me]

    def wait_att(off, carry):
        source = slot_of(lax.rem(me + off, n))
        pltpu.make_async_remote_copy(
            src_ref=att_send.at[0],
            dst_ref=att_recv.at[source],
            send_sem=att_ssem.at[off],
            recv_sem=att_rsem.at[source],
            device_id={"dev": twin},
            device_id_type=MESH,
        ).wait_recv()
        return carry

    lax.fori_loop(1, n, wait_att, 0)
    att_wide[...] = att_recv[...].astype(F32).reshape(att_wide.shape)
    for k in range(2 * heads_dev):
        lhs[:, k * 128 : (k + 1) * 128] = att_wide[pl.ds(k, rows, stride=8), :].astype(BF16)

    half_rows, quarter_rows = n * 8, n * 4

    def groups_of(count):
        edges = [chunks * g // count for g in range(count + 1)]
        return [(a, b - a) for a, b in zip(edges[:-1], edges[1:])]

    rs_groups = groups_of(min(RS_GROUPS, chunks))
    ag_groups = groups_of(min(AG_GROUPS, chunks))

    def move(src, dst, ssem, rsem, peer):
        return pltpu.make_async_remote_copy(
            src_ref=src,
            dst_ref=dst,
            send_sem=ssem,
            recv_sem=rsem,
            device_id={"dev": peer},
            device_id_type=MESH,
        )

    def reduce_rows(turn, product):
        def to_twin(g):
            c, size = g
            part_of = (turn, pl.ds(c, size))
            return move(
                send1.at[part_of], recv1.at[part_of], s1_sem.at[turn, c], r1_sem.at[turn, c], twin
            )

        def to_y(g):
            c, size = g
            part_of = (turn, pl.ds(c, size))
            return move(
                send2.at[part_of], recv2.at[part_of], s2_sem.at[turn, c], r2_sem.at[turn, c], y_peer
            )

        def to_z(g, off):
            c, size = g
            other, peer = z_peer(off)
            return move(
                send3.at[turn, other, pl.ds(c, size)],
                recv3.at[turn, off, pl.ds(c, size)],
                s3_sem.at[turn, c, off],
                r3_sem.at[turn, c, off],
                peer,
            )

        def first(g):
            away = pl.multiple_of((1 - core) * half_rows, half_rows)
            for c in range(g[0], g[0] + g[1]):
                tile = product(c)
                for j in range(8):
                    part[c, pl.ds(j, rows, stride=8), :] = tile[:, j * 128 : (j + 1) * 128]
                send1[turn, c] = part[c, pl.ds(away, half_rows), :].astype(BF16)
            to_twin(g).start()

        def second(g):
            home = pl.multiple_of(core * half_rows, half_rows)
            away = pl.multiple_of((1 - y) * quarter_rows, quarter_rows)
            to_twin(g).wait_recv()
            for c in range(g[0], g[0] + g[1]):
                acc1[c] = part[c, pl.ds(home, half_rows), :] + recv1[turn, c].astype(F32)
                send2[turn, c] = acc1[c, pl.ds(away, quarter_rows), :].astype(BF16)
            to_y(g).start()

        def third(g):
            home = pl.multiple_of(y * quarter_rows, quarter_rows)
            to_y(g).wait_recv()
            for c in range(g[0], g[0] + g[1]):
                held = acc1[c, pl.ds(home, quarter_rows), :] + recv2[turn, c].astype(F32)
                held = held.reshape(nz, 16, 128)
                acc2[c] = held
                send3[turn, :, c] = held.astype(BF16)
            for off in range(1, nz):
                to_z(g, off).start()

        count = len(rs_groups)
        for step in range(count + 2):
            if step < count:
                first(rs_groups[step])
            if 0 <= step - 1 < count:
                second(rs_groups[step - 1])
            if 0 <= step - 2 < count:
                third(rs_groups[step - 2])
        sums = []
        for g in rs_groups:
            for off in range(1, nz):
                to_z(g, off).wait_recv()
            for c in range(g[0], g[0] + g[1]):
                total = acc2[c, z]
                for off in range(1, nz):
                    total = total + recv3[turn, off, c].astype(F32)
                sums.append(total)

        def finish():
            for g in rs_groups:
                to_twin(g).wait_send()
                to_y(g).wait_send()
                for off in range(1, nz):
                    to_z(g, off).wait_send()

        return sums, finish

    def project(c):
        wo_copies[c].wait()
        return jnp.dot(lhs[...], wo[:, columns(c)], preferred_element_type=F32)

    sums, finish_first = reduce_rows(0, project)
    square = jnp.zeros((16, 128), F32)
    for c in range(chunks):
        row = res_ref[c].astype(F32) + sums[c]
        state[c] = row
        square = square + row * row
    scale0 = lax.rsqrt(jnp.sum(square[:8], keepdims=True) / width + 1e-06)
    scale1 = lax.rsqrt(jnp.sum(square[8:], keepdims=True) / width + 1e-06)
    scale = jnp.concatenate(
        [jnp.broadcast_to(scale0, (8, 128)), jnp.broadcast_to(scale1, (8, 128))], axis=0
    )

    my_rows = pl.multiple_of(my_slot * 16, 16)
    y_rows = pl.multiple_of((core * 2 + y) * quarter_rows, quarter_rows)
    core_rows = pl.multiple_of(core * half_rows, half_rows)
    y_in_rows = pl.multiple_of((core * 2 + 1 - y) * quarter_rows, quarter_rows)
    core_in_rows = pl.multiple_of((1 - core) * half_rows, half_rows)

    def block_of_rows(g, start, size):
        return rows_all.at[pl.ds(g[0], g[1]), pl.ds(start, size)]

    def spread_z(g, off):
        block = block_of_rows(g, my_rows, 16)
        return move(block, block, gz_ssem.at[g[0], off], gz_rsem.at[g[0], off], z_peer(off)[1])

    def landed_z(g, off):
        source = lax.rem(z + nz - off, nz)
        block = block_of_rows(g, pl.multiple_of(y_rows + source * 16, 16), 16)
        return move(block, block, gz_ssem.at[g[0], off], gz_rsem.at[g[0], off], z_peer(off)[1])

    def spread_y(g, start):
        block = block_of_rows(g, start, quarter_rows)
        return move(block, block, gy_ssem.at[g[0]], gy_rsem.at[g[0]], y_peer)

    def spread_core(g, start):
        block = block_of_rows(g, start, half_rows)
        return move(block, block, gc_ssem.at[g[0]], gc_rsem.at[g[0]], twin)

    for g in ag_groups:
        for c in range(g[0], g[0] + g[1]):
            gain = gain_ref[c].astype(F32)
            gain = jnp.concatenate([gain, gain], axis=0)
            rows_all[c, pl.ds(my_rows, 16), :] = (state[c] * scale * gain).astype(BF16)
        for off in range(1, nz):
            spread_z(g, off).start()

    gate = jnp.zeros((rows, wg.shape[0]), F32)
    up = jnp.zeros((rows, wg.shape[0]), F32)
    count = len(ag_groups)
    for step in range(count + 2):
        if step < count:
            g = ag_groups[step]
            for off in range(1, nz):
                landed_z(g, off).wait_recv()
            spread_y(g, y_rows).start()
        if 0 <= step - 1 < count:
            g = ag_groups[step - 1]
            spread_y(g, y_in_rows).wait_recv()
            spread_core(g, core_rows).start()
        if 0 <= step - 2 < count:
            g = ag_groups[step - 2]
            spread_core(g, core_in_rows).wait_recv()
            for c in range(g[0], g[0] + g[1]):
                rows_wide[...] = rows_all[c].astype(F32)
                for j in range(8):
                    normed[:, j * 128 : (j + 1) * 128] = rows_wide[
                        pl.ds(j, rows, stride=8), :
                    ].astype(BF16)
                held = normed[...]
                wg_copies[c].wait()
                wu_copies[c].wait()
                gate = gate + lax.dot_general(
                    held, wg[:, columns(c)], contract_last, preferred_element_type=F32
                )
                up = up + lax.dot_general(
                    held, wu[:, columns(c)], contract_last, preferred_element_type=F32
                )

    hidden = (gate / (1.0 + jnp.exp(-gate)) * up).astype(BF16)

    def down(c):
        wd_copies[c].wait()
        return jnp.dot(hidden, wd[:, columns(c)], preferred_element_type=F32)

    sums, finish_second = reduce_rows(1, down)
    for c in range(chunks):
        out_ref[c] = state[c] + sums[c]

    def drain_att(off, carry):
        att_copy(off).wait_send()
        return carry

    lax.fori_loop(1, n, drain_att, 0)
    finish_first()
    finish_second()
    for g in ag_groups:
        for off in range(1, nz):
            spread_z(g, off).wait_send()
        spread_y(g, y_rows).wait_send()
        spread_core(g, core_rows).wait_send()


def per_device(
    n,
    kv_pool,
    block_table,
    lengths,
    queries,
    new_kv,
    residual_in,
    norm_gain,
    out_weight,
    gate_weight,
    up_weight,
    down_weight,
):
    steps = queries.shape[0]
    head_width = new_kv.shape[2] // 2
    head_count = queries.shape[2] // head_width
    heads_dev = head_count // n
    width = residual_in.shape[2]
    chunks = width // WIDE
    nz = n // 4
    positions = kv_pool.shape[0] * kv_pool.shape[1]

    q = (
        queries.reshape(steps, n, heads_dev, head_width)
        .transpose(2, 1, 0, 3)
        .reshape(head_count * steps, head_width)
    )
    fresh = jnp.pad(new_kv.reshape(steps, -1), ((0, 16 - steps), (0, 0)))
    residual = (
        residual_in.reshape(steps, chunks, 8, 128)
        .transpose(1, 0, 2, 3)
        .reshape(chunks, 8 * steps, 128)
    )
    gain = norm_gain.reshape(chunks, 8, 128)
    cache = kv_pool.reshape(positions, 2 * head_width)

    vmem = pl.BlockSpec(memory_space=pltpu.VMEM)
    smem = pl.BlockSpec(memory_space=pltpu.SMEM)
    hbm = pl.BlockSpec(memory_space=pl.ANY)
    dma = pltpu.SemaphoreType.DMA
    out = pl.pallas_call(
        functools.partial(layer_kernel, n),
        out_shape=jax.ShapeDtypeStruct((chunks, 16, 128), F32),
        in_specs=[smem, smem, vmem, vmem, vmem, vmem] + [hbm] * 5,
        out_specs=vmem,
        scratch_shapes=[
            pltpu.VMEM((positions, 2 * head_width), BF16),
            pltpu.VMEM(out_weight.shape, BF16),
            pltpu.VMEM(gate_weight.shape[::-1], BF16),
            pltpu.VMEM(up_weight.shape[::-1], BF16),
            pltpu.VMEM(down_weight.shape, BF16),
            pltpu.VMEM((n * 16, 128), F32),
            pltpu.VMEM((n, 16, 128), BF16),
            pltpu.VMEM((n, 16, 128), BF16),
            pltpu.VMEM((n * 16, 128), F32),
            pltpu.VMEM((2 * n, heads_dev * head_width), BF16),
            pltpu.VMEM((chunks, n * 16, 128), F32),
            pltpu.VMEM((2, chunks, n * 8, 128), BF16),
            pltpu.VMEM((2, chunks, n * 8, 128), BF16),
            pltpu.VMEM((chunks, n * 8, 128), F32),
            pltpu.VMEM((2, chunks, n * 4, 128), BF16),
            pltpu.VMEM((2, chunks, n * 4, 128), BF16),
            pltpu.VMEM((chunks, nz, 16, 128), F32),
            pltpu.VMEM((2, nz, chunks, 16, 128), BF16),
            pltpu.VMEM((2, nz, chunks, 16, 128), BF16),
            pltpu.VMEM((chunks, 16, 128), F32),
            pltpu.VMEM((chunks, n * 16, 128), BF16),
            pltpu.VMEM((n * 16, 128), F32),
            pltpu.VMEM((2 * n, WIDE), BF16),
            dma(()),
            dma((4, chunks)),
            dma((n,)),
            dma((n,)),
            dma((2, chunks)),
            dma((2, chunks)),
            dma((2, chunks)),
            dma((2, chunks)),
            dma((2, chunks, nz)),
            dma((2, chunks, nz)),
            dma((chunks, nz)),
            dma((chunks, nz)),
            dma((chunks,)),
            dma((chunks,)),
            dma((chunks,)),
            dma((chunks,)),
        ],
        compiler_params=pltpu.CompilerParams(
            collective_id=0, has_side_effects=True, vmem_limit_bytes=60 * 1024 * 1024
        ),
        cost_estimate=pl.CostEstimate(
            flops=2 * 2 * n * (out_weight.size + 3 * gate_weight.size),
            bytes_accessed=2 * (out_weight.size + 3 * gate_weight.size + cache.size),
            transcendentals=0,
        ),
        name="decode_layer",
    )(
        block_table,
        lengths,
        q,
        fresh,
        residual,
        gain,
        cache,
        out_weight,
        gate_weight.T,
        up_weight.T,
        down_weight,
    )
    return (
        out.reshape(chunks, steps, 8, 128).transpose(1, 0, 2, 3).reshape(steps, 1, width)
    )


def solution(mesh):
    placed = (
        P(("grp", "dev"), None, None),
        P(("grp", "dev"), None),
        P(("grp", "dev")),
        P(None, ("grp", "dev"), None),
        P(None, ("grp", "dev"), None),
        P(None, ("grp", "dev"), None),
        P(),
        P("dev", None),
        P(None, "dev"),
        P(None, "dev"),
        P("dev", None),
    )
    return jax.shard_map(
        functools.partial(per_device, mesh.shape["dev"]),
        mesh=mesh,
        in_specs=placed,
        out_specs=P(None, ("grp", "dev"), None),
        check_vma=False,
    )
```

```python
import functools

import jax
import jax.numpy as jnp
from jax import lax
from jax.experimental import pallas as pl
from jax.experimental.pallas import tpu as pltpu
from jax.sharding import PartitionSpec as P

F32 = jnp.float32
BF16 = jnp.bfloat16
MESH = pl.DeviceIdType.MESH
RS_GROUPS = 2
AG_GROUPS = 2
WIDE = 1024


def layer_kernel(
    n,
    table_ref,
    length_ref,
    q_ref,
    fresh_ref,
    res_ref,
    gain_ref,
    kv_hbm,
    wo_hbm,
    wg_hbm,
    wu_hbm,
    wd_hbm,
    out_ref,
    kv,
    wo,
    wg,
    wu,
    wd,
    att,
    att_send,
    att_recv,
    att_wide,
    lhs,
    part,
    send1,
    recv1,
    acc1,
    send2,
    recv2,
    acc2,
    send3,
    recv3,
    state,
    rows_all,
    rows_wide,
    normed,
    q_wide,
    res,
    fresh_wide,
    kv_sem,
    w_sem,
    att_ssem,
    att_rsem,
    s1_sem,
    r1_sem,
    s2_sem,
    r2_sem,
    s3_sem,
    r3_sem,
    gz_ssem,
    gz_rsem,
    gy_ssem,
    gy_rsem,
    gc_ssem,
    gc_rsem,
):
    me = lax.axis_index("dev")
    nz = n // 4
    core, y, z = lax.rem(me, 2), lax.rem(me // 2, 2), me // 4
    chunks = state.shape[0]
    heads_dev = lhs.shape[1] // 256
    rows = 2 * n
    width = chunks * WIDE

    def slot_of(i):
        return lax.rem(i, 2) * (n // 2) + lax.rem(i // 2, 2) * nz + i // 4

    my_slot = slot_of(me)
    twin = me + 1 - 2 * core
    y_peer = me + 2 - 4 * y

    def z_peer(off):
        other = lax.rem(z + off, nz)
        return other, other * 4 + y * 2 + core

    key_copy = pltpu.make_async_copy(kv_hbm.at[:, :256], kv.at[:, :256], kv_sem.at[0])
    value_copy = pltpu.make_async_copy(kv_hbm.at[:, 256:], kv.at[:, 256:], kv_sem.at[1])
    key_copy.start()
    value_copy.start()

    def columns(c):
        return pl.ds(c * WIDE, WIDE)

    wo_copies = [
        pltpu.make_async_copy(wo_hbm.at[:, columns(c)], wo.at[:, columns(c)], w_sem.at[0, c])
        for c in range(chunks)
    ]
    wg_copies = [
        pltpu.make_async_copy(wg_hbm.at[:, columns(c)], wg.at[:, columns(c)], w_sem.at[1, c])
        for c in range(chunks)
    ]
    wu_copies = [
        pltpu.make_async_copy(wu_hbm.at[:, columns(c)], wu.at[:, columns(c)], w_sem.at[2, c])
        for c in range(chunks)
    ]
    wd_copies = [
        pltpu.make_async_copy(wd_hbm.at[:, columns(c)], wd.at[:, columns(c)], w_sem.at[3, c])
        for c in range(chunks)
    ]

    barrier = pltpu.get_barrier_semaphore()

    def greet(off, carry):
        pl.semaphore_signal(
            barrier, inc=1, device_id={"dev": lax.rem(me + off, n)}, device_id_type=MESH
        )
        return carry

    lax.fori_loop(1, n, greet, 0)

    positions = kv.shape[0]
    blocks = table_ref.shape[1]
    block_rows = positions // blocks
    place = lax.broadcasted_iota(jnp.int32, (1, positions), 1)
    block_of = place // block_rows
    order = jnp.zeros((1, positions), jnp.int32)
    for j in range(blocks):
        order = jnp.where(block_of == lax.rem(table_ref[0, j], blocks), j, order)
    position = order * block_rows + (place - block_of * block_rows)
    visible = position < length_ref[0]

    for h in range(heads_dev):
        for i in range(n):
            at = (i * heads_dev + h) * 256
            q_wide[pl.ds(h * rows + i * 2, 2), :] = q_ref[:, at : at + 256].astype(F32)
    for c in range(chunks):
        for j in range(8):
            at = c * WIDE + j * 128
            res[c, pl.ds(j, 2, stride=8), :] = res_ref[:, at : at + 128].astype(F32)
    fresh_wide[...] = jnp.zeros_like(fresh_wide)
    fresh_wide[pl.ds(0, 2), :] = fresh_ref[...].astype(F32)
    q = q_wide[...].astype(BF16)
    q_rows = q.shape[0]
    contract_last = (((1,), (1,)), ((), ()))
    fresh = fresh_wide[...].astype(BF16)
    fresh_scores = (
        lax.dot_general(q, fresh[:, :256], contract_last, preferred_element_type=F32) * 0.0625
    )
    step_of_row = lax.rem(lax.broadcasted_iota(jnp.int32, (q_rows, 16), 0), 2)
    fresh_step = lax.broadcasted_iota(jnp.int32, (q_rows, 16), 1)
    fresh_scores = jnp.where(fresh_step <= step_of_row, fresh_scores, -jnp.inf)
    key_copy.wait()
    for copy in wo_copies:
        copy.start()
    scores = (
        lax.dot_general(q, kv[:, :256], contract_last, preferred_element_type=F32) * 0.0625
    )
    scores = jnp.where(visible, scores, -jnp.inf)
    largest = jnp.maximum(
        jnp.max(scores, axis=1, keepdims=True), jnp.max(fresh_scores, axis=1, keepdims=True)
    )
    weights = jnp.exp(scores - largest)
    fresh_weights = jnp.exp(fresh_scores - largest)
    total = jnp.sum(weights, axis=1, keepdims=True) + jnp.sum(
        fresh_weights, axis=1, keepdims=True
    )
    value_copy.wait()
    for pair in zip(wg_copies, wu_copies):
        for copy in pair:
            copy.start()
    probs = (weights / total).astype(BF16)
    fresh_probs = (fresh_weights / total).astype(BF16)
    attended = jnp.dot(probs, kv[:, 256:], preferred_element_type=F32) + jnp.dot(
        fresh_probs, fresh[:, 256:], preferred_element_type=F32
    )
    if heads_dev < 4:
        att[...] = jnp.zeros_like(att)
    for h in range(heads_dev):
        for half in range(2):
            att[pl.ds(h * 2 + half, rows, stride=8), :] = attended[
                h * rows : (h + 1) * rows, half * 128 : (half + 1) * 128
            ]
    att_send[...] = att[...].astype(BF16).reshape(att_send.shape)

    pl.semaphore_wait(barrier, n - 1)

    def att_copy(off):
        peer = lax.rem(me + off, n)
        return pltpu.make_async_remote_copy(
            src_ref=att_send.at[peer],
            dst_ref=att_recv.at[my_slot],
            send_sem=att_ssem.at[off],
            recv_sem=att_rsem.at[my_slot],
            device_id={"dev": peer},
            device_id_type=MESH,
        )

    def start_att(off, carry):
        att_copy(off).start()
        return carry

    lax.fori_loop(1, n, start_att, 0)
    att_recv[my_slot] = att_send[me]

    def wait_att(off, carry):
        source = slot_of(lax.rem(me + off, n))
        pltpu.make_async_remote_copy(
            src_ref=att_send.at[0],
            dst_ref=att_recv.at[source],
            send_sem=att_ssem.at[off],
            recv_sem=att_rsem.at[source],
            device_id={"dev": twin},
            device_id_type=MESH,
        ).wait_recv()
        return carry

    lax.fori_loop(1, n, wait_att, 0)
    att_wide[...] = att_recv[...].astype(F32).reshape(att_wide.shape)
    for k in range(2 * heads_dev):
        lhs[:, k * 128 : (k + 1) * 128] = att_wide[pl.ds(k, rows, stride=8), :].astype(BF16)

    half_rows, quarter_rows = n * 8, n * 4

    def groups_of(count):
        edges = [chunks * g // count for g in range(count + 1)]
        return [(a, b - a) for a, b in zip(edges[:-1], edges[1:])]

    rs_groups = groups_of(min(RS_GROUPS, chunks))
    ag_groups = groups_of(min(AG_GROUPS, chunks))

    def move(src, dst, ssem, rsem, peer):
        return pltpu.make_async_remote_copy(
            src_ref=src,
            dst_ref=dst,
            send_sem=ssem,
            recv_sem=rsem,
            device_id={"dev": peer},
            device_id_type=MESH,
        )

    def reduce_rows(turn, product):
        def to_twin(g):
            c, size = g
            part_of = (turn, pl.ds(c, size))
            return move(
                send1.at[part_of], recv1.at[part_of], s1_sem.at[turn, c], r1_sem.at[turn, c], twin
            )

        def to_y(g):
            c, size = g
            part_of = (turn, pl.ds(c, size))
            return move(
                send2.at[part_of], recv2.at[part_of], s2_sem.at[turn, c], r2_sem.at[turn, c], y_peer
            )

        def to_z(g, off):
            c, size = g
            other, peer = z_peer(off)
            return move(
                send3.at[turn, other, pl.ds(c, size)],
                recv3.at[turn, off, pl.ds(c, size)],
                s3_sem.at[turn, c, off],
                r3_sem.at[turn, c, off],
                peer,
            )

        def first(g):
            away = pl.multiple_of((1 - core) * half_rows, half_rows)
            for c in range(g[0], g[0] + g[1]):
                tile = product(c)
                for j in range(8):
                    part[c, pl.ds(j, rows, stride=8), :] = tile[:, j * 128 : (j + 1) * 128]
                send1[turn, c] = part[c, pl.ds(away, half_rows), :].astype(BF16)
            to_twin(g).start()

        def second(g):
            home = pl.multiple_of(core * half_rows, half_rows)
            away = pl.multiple_of((1 - y) * quarter_rows, quarter_rows)
            to_twin(g).wait_recv()
            for c in range(g[0], g[0] + g[1]):
                acc1[c] = part[c, pl.ds(home, half_rows), :] + recv1[turn, c].astype(F32)
                send2[turn, c] = acc1[c, pl.ds(away, quarter_rows), :].astype(BF16)
            to_y(g).start()

        def third(g):
            home = pl.multiple_of(y * quarter_rows, quarter_rows)
            to_y(g).wait_recv()
            for c in range(g[0], g[0] + g[1]):
                held = acc1[c, pl.ds(home, quarter_rows), :] + recv2[turn, c].astype(F32)
                held = held.reshape(nz, 16, 128)
                acc2[c] = held
                send3[turn, :, c] = held.astype(BF16)
            for off in range(1, nz):
                to_z(g, off).start()

        count = len(rs_groups)
        for step in range(count + 2):
            if step < count:
                first(rs_groups[step])
            if 0 <= step - 1 < count:
                second(rs_groups[step - 1])
            if 0 <= step - 2 < count:
                third(rs_groups[step - 2])
        sums = []
        for g in rs_groups:
            for off in range(1, nz):
                to_z(g, off).wait_recv()
            for c in range(g[0], g[0] + g[1]):
                total = acc2[c, z]
                for off in range(1, nz):
                    total = total + recv3[turn, off, c].astype(F32)
                sums.append(total)

        def finish():
            for g in rs_groups:
                to_twin(g).wait_send()
                to_y(g).wait_send()
                for off in range(1, nz):
                    to_z(g, off).wait_send()

        return sums, finish

    def project(c):
        wo_copies[c].wait()
        return jnp.dot(lhs[...], wo[:, columns(c)], preferred_element_type=F32)

    for copy in wd_copies:
        copy.start()
    sums, finish_first = reduce_rows(0, project)
    square = jnp.zeros((16, 128), F32)
    for c in range(chunks):
        row = res[c] + sums[c]
        state[c] = row
        square = square + row * row
    scale0 = lax.rsqrt(jnp.sum(square[:8], keepdims=True) / width + 1e-06)
    scale1 = lax.rsqrt(jnp.sum(square[8:], keepdims=True) / width + 1e-06)
    scale = jnp.concatenate(
        [jnp.broadcast_to(scale0, (8, 128)), jnp.broadcast_to(scale1, (8, 128))], axis=0
    )

    my_rows = pl.multiple_of(my_slot * 16, 16)
    y_rows = pl.multiple_of((core * 2 + y) * quarter_rows, quarter_rows)
    core_rows = pl.multiple_of(core * half_rows, half_rows)
    y_in_rows = pl.multiple_of((core * 2 + 1 - y) * quarter_rows, quarter_rows)
    core_in_rows = pl.multiple_of((1 - core) * half_rows, half_rows)

    def block_of_rows(g, start, size):
        return rows_all.at[pl.ds(g[0], g[1]), pl.ds(start, size)]

    def spread_z(g, off):
        block = block_of_rows(g, my_rows, 16)
        return move(block, block, gz_ssem.at[g[0], off], gz_rsem.at[g[0], off], z_peer(off)[1])

    def landed_z(g, off):
        source = lax.rem(z + nz - off, nz)
        block = block_of_rows(g, pl.multiple_of(y_rows + source * 16, 16), 16)
        return move(block, block, gz_ssem.at[g[0], off], gz_rsem.at[g[0], off], z_peer(off)[1])

    def spread_y(g, start):
        block = block_of_rows(g, start, quarter_rows)
        return move(block, block, gy_ssem.at[g[0]], gy_rsem.at[g[0]], y_peer)

    def spread_core(g, start):
        block = block_of_rows(g, start, half_rows)
        return move(block, block, gc_ssem.at[g[0]], gc_rsem.at[g[0]], twin)

    for g in ag_groups:
        for c in range(g[0], g[0] + g[1]):
            gain = gain_ref[c].astype(F32)
            gain = jnp.concatenate([gain, gain], axis=0)
            rows_all[c, pl.ds(my_rows, 16), :] = (state[c] * scale * gain).astype(BF16)
        for off in range(1, nz):
            spread_z(g, off).start()

    gate = jnp.zeros((rows, wg.shape[0]), F32)
    up = jnp.zeros((rows, wg.shape[0]), F32)
    count = len(ag_groups)
    for step in range(count + 2):
        if step < count:
            g = ag_groups[step]
            for off in range(1, nz):
                landed_z(g, off).wait_recv()
            spread_y(g, y_rows).start()
        if 0 <= step - 1 < count:
            g = ag_groups[step - 1]
            spread_y(g, y_in_rows).wait_recv()
            spread_core(g, core_rows).start()
        if 0 <= step - 2 < count:
            g = ag_groups[step - 2]
            spread_core(g, core_in_rows).wait_recv()
            for c in range(g[0], g[0] + g[1]):
                rows_wide[...] = rows_all[c].astype(F32)
                for j in range(8):
                    normed[:, j * 128 : (j + 1) * 128] = rows_wide[
                        pl.ds(j, rows, stride=8), :
                    ].astype(BF16)
                held = normed[...]
                wg_copies[c].wait()
                wu_copies[c].wait()
                gate = gate + lax.dot_general(
                    held, wg[:, columns(c)], contract_last, preferred_element_type=F32
                )
                up = up + lax.dot_general(
                    held, wu[:, columns(c)], contract_last, preferred_element_type=F32
                )

    hidden = (gate / (1.0 + jnp.exp(-gate)) * up).astype(BF16)

    def down(c):
        wd_copies[c].wait()
        return jnp.dot(hidden, wd[:, columns(c)], preferred_element_type=F32)

    sums, finish_second = reduce_rows(1, down)
    for c in range(chunks):
        out_ref[c] = state[c] + sums[c]

    def drain_att(off, carry):
        att_copy(off).wait_send()
        return carry

    lax.fori_loop(1, n, drain_att, 0)
    finish_first()
    finish_second()
    for g in ag_groups:
        for off in range(1, nz):
            spread_z(g, off).wait_send()
        spread_y(g, y_rows).wait_send()
        spread_core(g, core_rows).wait_send()


def per_device(
    n,
    kv_pool,
    block_table,
    lengths,
    queries,
    new_kv,
    residual_in,
    norm_gain,
    out_weight,
    gate_weight,
    up_weight,
    down_weight,
):
    steps = queries.shape[0]
    head_width = new_kv.shape[2] // 2
    head_count = queries.shape[2] // head_width
    heads_dev = head_count // n
    width = residual_in.shape[2]
    chunks = width // WIDE
    nz = n // 4
    positions = kv_pool.shape[0] * kv_pool.shape[1]

    q = queries.reshape(steps, -1)
    fresh = new_kv.reshape(steps, -1)
    residual = residual_in.reshape(steps, -1)
    gain = norm_gain.reshape(chunks, 8, 128)
    cache = kv_pool.reshape(positions, 2 * head_width)

    vmem = pl.BlockSpec(memory_space=pltpu.VMEM)
    smem = pl.BlockSpec(memory_space=pltpu.SMEM)
    hbm = pl.BlockSpec(memory_space=pl.ANY)
    dma = pltpu.SemaphoreType.DMA
    out = pl.pallas_call(
        functools.partial(layer_kernel, n),
        out_shape=jax.ShapeDtypeStruct((chunks, 16, 128), F32),
        in_specs=[smem, smem, vmem, vmem, vmem, vmem] + [hbm] * 5,
        out_specs=vmem,
        scratch_shapes=[
            pltpu.VMEM((positions, 2 * head_width), BF16),
            pltpu.VMEM(out_weight.shape, BF16),
            pltpu.VMEM(gate_weight.shape[::-1], BF16),
            pltpu.VMEM(up_weight.shape[::-1], BF16),
            pltpu.VMEM(down_weight.shape, BF16),
            pltpu.VMEM((n * 16, 128), F32),
            pltpu.VMEM((n, 16, 128), BF16),
            pltpu.VMEM((n, 16, 128), BF16),
            pltpu.VMEM((n * 16, 128), F32),
            pltpu.VMEM((2 * n, heads_dev * head_width), BF16),
            pltpu.VMEM((chunks, n * 16, 128), F32),
            pltpu.VMEM((2, chunks, n * 8, 128), BF16),
            pltpu.VMEM((2, chunks, n * 8, 128), BF16),
            pltpu.VMEM((chunks, n * 8, 128), F32),
            pltpu.VMEM((2, chunks, n * 4, 128), BF16),
            pltpu.VMEM((2, chunks, n * 4, 128), BF16),
            pltpu.VMEM((chunks, nz, 16, 128), F32),
            pltpu.VMEM((2, nz, chunks, 16, 128), BF16),
            pltpu.VMEM((2, nz, chunks, 16, 128), BF16),
            pltpu.VMEM((chunks, 16, 128), F32),
            pltpu.VMEM((chunks, n * 16, 128), BF16),
            pltpu.VMEM((n * 16, 128), F32),
            pltpu.VMEM((2 * n, WIDE), BF16),
            pltpu.VMEM((head_count * steps, head_width), F32),
            pltpu.VMEM((chunks, 16, 128), F32),
            pltpu.VMEM((16, 2 * head_width), F32),
            dma((2,)),
            dma((4, chunks)),
            dma((n,)),
            dma((n,)),
            dma((2, chunks)),
            dma((2, chunks)),
            dma((2, chunks)),
            dma((2, chunks)),
            dma((2, chunks, nz)),
            dma((2, chunks, nz)),
            dma((chunks, nz)),
            dma((chunks, nz)),
            dma((chunks,)),
            dma((chunks,)),
            dma((chunks,)),
            dma((chunks,)),
        ],
        compiler_params=pltpu.CompilerParams(
            collective_id=0, has_side_effects=True, vmem_limit_bytes=60 * 1024 * 1024
        ),
        cost_estimate=pl.CostEstimate(
            flops=2 * 2 * n * (out_weight.size + 3 * gate_weight.size),
            bytes_accessed=2 * (out_weight.size + 3 * gate_weight.size + cache.size),
            transcendentals=0,
        ),
        name="decode_layer",
    )(
        block_table,
        lengths,
        q,
        fresh,
        residual,
        gain,
        cache,
        out_weight,
        gate_weight.T,
        up_weight.T,
        down_weight,
    )
    return (
        out.reshape(chunks, steps, 8, 128).transpose(1, 0, 2, 3).reshape(steps, 1, width)
    )


def solution(mesh):
    placed = (
        P(("grp", "dev"), None, None),
        P(("grp", "dev"), None),
        P(("grp", "dev")),
        P(None, ("grp", "dev"), None),
        P(None, ("grp", "dev"), None),
        P(None, ("grp", "dev"), None),
        P(),
        P("dev", None),
        P(None, "dev"),
        P(None, "dev"),
        P("dev", None),
    )
    return jax.shard_map(
        functools.partial(per_device, mesh.shape["dev"]),
        mesh=mesh,
        in_specs=placed,
        out_specs=P(None, ("grp", "dev"), None),
        check_vma=False,
    )
```

```python
import functools

import jax
import jax.numpy as jnp
from jax import lax
from jax.experimental import pallas as pl
from jax.experimental.pallas import tpu as pltpu
from jax.sharding import PartitionSpec as P

F32 = jnp.float32
BF16 = jnp.bfloat16
MESH = pl.DeviceIdType.MESH
RS_GROUPS = 2
AG_GROUPS = 2
WIDE = 1024


def layer_kernel(
    n,
    table_ref,
    length_ref,
    q_ref,
    fresh_ref,
    res_ref,
    gain_ref,
    kv_hbm,
    wo_hbm,
    wg_hbm,
    wu_hbm,
    wd_hbm,
    out_ref,
    kv,
    wo,
    wg,
    wu,
    wd,
    att,
    att_send,
    att_recv,
    att_wide,
    lhs,
    part,
    send1,
    recv1,
    acc1,
    send2,
    recv2,
    acc2,
    send3,
    recv3,
    state,
    rows_all,
    rows_wide,
    normed,
    q_wide,
    res,
    fresh_wide,
    kv_sem,
    w_sem,
    att_ssem,
    att_rsem,
    s1_sem,
    r1_sem,
    s2_sem,
    r2_sem,
    s3_sem,
    r3_sem,
    gz_ssem,
    gz_rsem,
    gy_ssem,
    gy_rsem,
    gc_ssem,
    gc_rsem,
):
    me = lax.axis_index("dev")
    nz = n // 4
    core, y, z = lax.rem(me, 2), lax.rem(me // 2, 2), me // 4
    chunks = state.shape[0]
    heads_dev = lhs.shape[1] // 256
    rows = 2 * n
    width = chunks * WIDE

    def slot_of(i):
        return lax.rem(i, 2) * (n // 2) + lax.rem(i // 2, 2) * nz + i // 4

    my_slot = slot_of(me)
    twin = me + 1 - 2 * core
    y_peer = me + 2 - 4 * y

    def z_peer(off):
        other = lax.rem(z + off, nz)
        return other, other * 4 + y * 2 + core

    key_copy = pltpu.make_async_copy(kv_hbm.at[:, :256], kv.at[:, :256], kv_sem.at[0])
    value_copy = pltpu.make_async_copy(kv_hbm.at[:, 256:], kv.at[:, 256:], kv_sem.at[1])
    key_copy.start()
    value_copy.start()

    def columns(c):
        return pl.ds(c * WIDE, WIDE)

    wo_copies = [
        pltpu.make_async_copy(wo_hbm.at[:, columns(c)], wo.at[:, columns(c)], w_sem.at[0, c])
        for c in range(chunks)
    ]
    wg_copies = [
        pltpu.make_async_copy(wg_hbm.at[:, columns(c)], wg.at[:, columns(c)], w_sem.at[1, c])
        for c in range(chunks)
    ]
    wu_copies = [
        pltpu.make_async_copy(wu_hbm.at[:, columns(c)], wu.at[:, columns(c)], w_sem.at[2, c])
        for c in range(chunks)
    ]
    wd_copies = [
        pltpu.make_async_copy(wd_hbm.at[:, columns(c)], wd.at[:, columns(c)], w_sem.at[3, c])
        for c in range(chunks)
    ]

    barrier = pltpu.get_barrier_semaphore()

    def greet(off, carry):
        pl.semaphore_signal(
            barrier, inc=1, device_id={"dev": lax.rem(me + off, n)}, device_id_type=MESH
        )
        return carry

    lax.fori_loop(1, n, greet, 0)

    positions = kv.shape[0]
    blocks = table_ref.shape[1]
    block_rows = positions // blocks
    place = lax.broadcasted_iota(jnp.int32, (1, positions), 1)
    block_of = place // block_rows
    order = jnp.zeros((1, positions), jnp.int32)
    for j in range(blocks):
        order = jnp.where(block_of == lax.rem(table_ref[0, j], blocks), j, order)
    position = order * block_rows + (place - block_of * block_rows)
    visible = position < length_ref[0]

    for h in range(heads_dev):
        for i in range(n):
            at = (i * heads_dev + h) * 256
            q_wide[pl.ds(h * rows + i * 2, 2), :] = q_ref[:, at : at + 256].astype(F32)
    fresh_wide[...] = jnp.zeros_like(fresh_wide)
    fresh_wide[pl.ds(0, 2), :] = fresh_ref[...].astype(F32)
    q = q_wide[...].astype(BF16)
    q_rows = q.shape[0]
    contract_last = (((1,), (1,)), ((), ()))
    fresh = fresh_wide[...].astype(BF16)
    fresh_scores = (
        lax.dot_general(q, fresh[:, :256], contract_last, preferred_element_type=F32) * 0.0625
    )
    step_of_row = lax.rem(lax.broadcasted_iota(jnp.int32, (q_rows, 16), 0), 2)
    fresh_step = lax.broadcasted_iota(jnp.int32, (q_rows, 16), 1)
    fresh_scores = jnp.where(fresh_step <= step_of_row, fresh_scores, -jnp.inf)
    key_copy.wait()
    for copy in wo_copies:
        copy.start()
    scores = (
        lax.dot_general(q, kv[:, :256], contract_last, preferred_element_type=F32) * 0.0625
    )
    scores = jnp.where(visible, scores, -jnp.inf)
    largest = jnp.maximum(
        jnp.max(scores, axis=1, keepdims=True), jnp.max(fresh_scores, axis=1, keepdims=True)
    )
    weights = jnp.exp(scores - largest)
    fresh_weights = jnp.exp(fresh_scores - largest)
    total = jnp.sum(weights, axis=1, keepdims=True) + jnp.sum(
        fresh_weights, axis=1, keepdims=True
    )
    value_copy.wait()
    share = 1.0 / total
    for pair in zip(wg_copies, wu_copies):
        for copy in pair:
            copy.start()
    probs = (weights * share).astype(BF16)
    fresh_probs = (fresh_weights * share).astype(BF16)
    attended = jnp.dot(probs, kv[:, 256:], preferred_element_type=F32) + jnp.dot(
        fresh_probs, fresh[:, 256:], preferred_element_type=F32
    )
    if heads_dev < 4:
        att[...] = jnp.zeros_like(att)
    for h in range(heads_dev):
        for half in range(2):
            att[pl.ds(h * 2 + half, rows, stride=8), :] = attended[
                h * rows : (h + 1) * rows, half * 128 : (half + 1) * 128
            ]
    att_send[...] = att[...].astype(BF16).reshape(att_send.shape)

    pl.semaphore_wait(barrier, n - 1)

    def att_copy(off):
        peer = lax.rem(me + off, n)
        return pltpu.make_async_remote_copy(
            src_ref=att_send.at[peer],
            dst_ref=att_recv.at[my_slot],
            send_sem=att_ssem.at[off],
            recv_sem=att_rsem.at[my_slot],
            device_id={"dev": peer},
            device_id_type=MESH,
        )

    def start_att(off, carry):
        att_copy(off).start()
        return carry

    lax.fori_loop(1, n, start_att, 0)
    att_recv[my_slot] = att_send[me]
    for c in range(chunks):
        for j in range(8):
            at = c * WIDE + j * 128
            res[c, pl.ds(j, 2, stride=8), :] = res_ref[:, at : at + 128].astype(F32)

    def wait_att(off, carry):
        source = slot_of(lax.rem(me + off, n))
        pltpu.make_async_remote_copy(
            src_ref=att_send.at[0],
            dst_ref=att_recv.at[source],
            send_sem=att_ssem.at[off],
            recv_sem=att_rsem.at[source],
            device_id={"dev": twin},
            device_id_type=MESH,
        ).wait_recv()
        return carry

    lax.fori_loop(1, n, wait_att, 0)
    att_wide[...] = att_recv[...].astype(F32).reshape(att_wide.shape)
    for k in range(2 * heads_dev):
        lhs[:, k * 128 : (k + 1) * 128] = att_wide[pl.ds(k, rows, stride=8), :].astype(BF16)

    half_rows, quarter_rows = n * 8, n * 4

    def groups_of(count):
        edges = [chunks * g // count for g in range(count + 1)]
        return [(a, b - a) for a, b in zip(edges[:-1], edges[1:])]

    rs_groups = groups_of(min(RS_GROUPS, chunks))
    ag_groups = groups_of(min(AG_GROUPS, chunks))

    def move(src, dst, ssem, rsem, peer):
        return pltpu.make_async_remote_copy(
            src_ref=src,
            dst_ref=dst,
            send_sem=ssem,
            recv_sem=rsem,
            device_id={"dev": peer},
            device_id_type=MESH,
        )

    def reduce_rows(turn, product):
        def to_twin(g):
            c, size = g
            part_of = (turn, pl.ds(c, size))
            return move(
                send1.at[part_of], recv1.at[part_of], s1_sem.at[turn, c], r1_sem.at[turn, c], twin
            )

        def to_y(g):
            c, size = g
            part_of = (turn, pl.ds(c, size))
            return move(
                send2.at[part_of], recv2.at[part_of], s2_sem.at[turn, c], r2_sem.at[turn, c], y_peer
            )

        def to_z(g, off):
            c, size = g
            other, peer = z_peer(off)
            return move(
                send3.at[turn, other, pl.ds(c, size)],
                recv3.at[turn, off, pl.ds(c, size)],
                s3_sem.at[turn, c, off],
                r3_sem.at[turn, c, off],
                peer,
            )

        def first(g):
            away = pl.multiple_of((1 - core) * half_rows, half_rows)
            for c in range(g[0], g[0] + g[1]):
                tile = product(c)
                for j in range(8):
                    part[c, pl.ds(j, rows, stride=8), :] = tile[:, j * 128 : (j + 1) * 128]
                send1[turn, c] = part[c, pl.ds(away, half_rows), :].astype(BF16)
            to_twin(g).start()

        def second(g):
            home = pl.multiple_of(core * half_rows, half_rows)
            away = pl.multiple_of((1 - y) * quarter_rows, quarter_rows)
            to_twin(g).wait_recv()
            for c in range(g[0], g[0] + g[1]):
                acc1[c] = part[c, pl.ds(home, half_rows), :] + recv1[turn, c].astype(F32)
                send2[turn, c] = acc1[c, pl.ds(away, quarter_rows), :].astype(BF16)
            to_y(g).start()

        def third(g):
            home = pl.multiple_of(y * quarter_rows, quarter_rows)
            to_y(g).wait_recv()
            for c in range(g[0], g[0] + g[1]):
                held = acc1[c, pl.ds(home, quarter_rows), :] + recv2[turn, c].astype(F32)
                held = held.reshape(nz, 16, 128)
                acc2[c] = held
                send3[turn, :, c] = held.astype(BF16)
            for off in range(1, nz):
                to_z(g, off).start()

        count = len(rs_groups)
        for step in range(count + 2):
            if step < count:
                first(rs_groups[step])
            if 0 <= step - 1 < count:
                second(rs_groups[step - 1])
            if 0 <= step - 2 < count:
                third(rs_groups[step - 2])
        sums = []
        for g in rs_groups:
            for off in range(1, nz):
                to_z(g, off).wait_recv()
            for c in range(g[0], g[0] + g[1]):
                total = acc2[c, z]
                for off in range(1, nz):
                    total = total + recv3[turn, off, c].astype(F32)
                sums.append(total)

        def finish():
            for g in rs_groups:
                to_twin(g).wait_send()
                to_y(g).wait_send()
                for off in range(1, nz):
                    to_z(g, off).wait_send()

        return sums, finish

    def project(c):
        wo_copies[c].wait()
        return jnp.dot(lhs[...], wo[:, columns(c)], preferred_element_type=F32)

    for copy in wd_copies:
        copy.start()
    sums, finish_first = reduce_rows(0, project)
    square = jnp.zeros((16, 128), F32)
    for c in range(chunks):
        row = res[c] + sums[c]
        state[c] = row
        square = square + row * row
    scale0 = lax.rsqrt(jnp.sum(square[:8], keepdims=True) / width + 1e-06)
    scale1 = lax.rsqrt(jnp.sum(square[8:], keepdims=True) / width + 1e-06)
    scale = jnp.concatenate(
        [jnp.broadcast_to(scale0, (8, 128)), jnp.broadcast_to(scale1, (8, 128))], axis=0
    )

    my_rows = pl.multiple_of(my_slot * 16, 16)
    y_rows = pl.multiple_of((core * 2 + y) * quarter_rows, quarter_rows)
    core_rows = pl.multiple_of(core * half_rows, half_rows)
    y_in_rows = pl.multiple_of((core * 2 + 1 - y) * quarter_rows, quarter_rows)
    core_in_rows = pl.multiple_of((1 - core) * half_rows, half_rows)

    def block_of_rows(g, start, size):
        return rows_all.at[pl.ds(g[0], g[1]), pl.ds(start, size)]

    def spread_z(g, off):
        block = block_of_rows(g, my_rows, 16)
        return move(block, block, gz_ssem.at[g[0], off], gz_rsem.at[g[0], off], z_peer(off)[1])

    def landed_z(g, off):
        source = lax.rem(z + nz - off, nz)
        block = block_of_rows(g, pl.multiple_of(y_rows + source * 16, 16), 16)
        return move(block, block, gz_ssem.at[g[0], off], gz_rsem.at[g[0], off], z_peer(off)[1])

    def spread_y(g, start):
        block = block_of_rows(g, start, quarter_rows)
        return move(block, block, gy_ssem.at[g[0]], gy_rsem.at[g[0]], y_peer)

    def spread_core(g, start):
        block = block_of_rows(g, start, half_rows)
        return move(block, block, gc_ssem.at[g[0]], gc_rsem.at[g[0]], twin)

    for g in ag_groups:
        for c in range(g[0], g[0] + g[1]):
            gain = gain_ref[c].astype(F32)
            gain = jnp.concatenate([gain, gain], axis=0)
            rows_all[c, pl.ds(my_rows, 16), :] = (state[c] * scale * gain).astype(BF16)
        for off in range(1, nz):
            spread_z(g, off).start()

    gate = jnp.zeros((rows, wg.shape[0]), F32)
    up = jnp.zeros((rows, wg.shape[0]), F32)
    count = len(ag_groups)
    for step in range(count + 2):
        if step < count:
            g = ag_groups[step]
            for off in range(1, nz):
                landed_z(g, off).wait_recv()
            spread_y(g, y_rows).start()
        if 0 <= step - 1 < count:
            g = ag_groups[step - 1]
            spread_y(g, y_in_rows).wait_recv()
            spread_core(g, core_rows).start()
        if 0 <= step - 2 < count:
            g = ag_groups[step - 2]
            spread_core(g, core_in_rows).wait_recv()
            for c in range(g[0], g[0] + g[1]):
                rows_wide[...] = rows_all[c].astype(F32)
                for j in range(8):
                    normed[:, j * 128 : (j + 1) * 128] = rows_wide[
                        pl.ds(j, rows, stride=8), :
                    ].astype(BF16)
                held = normed[...]
                wg_copies[c].wait()
                wu_copies[c].wait()
                gate = gate + lax.dot_general(
                    held, wg[:, columns(c)], contract_last, preferred_element_type=F32
                )
                up = up + lax.dot_general(
                    held, wu[:, columns(c)], contract_last, preferred_element_type=F32
                )

    hidden = (gate / (1.0 + jnp.exp(-gate)) * up).astype(BF16)

    def down(c):
        wd_copies[c].wait()
        return jnp.dot(hidden, wd[:, columns(c)], preferred_element_type=F32)

    sums, finish_second = reduce_rows(1, down)
    for c in range(chunks):
        out_ref[c] = state[c] + sums[c]

    def drain_att(off, carry):
        att_copy(off).wait_send()
        return carry

    lax.fori_loop(1, n, drain_att, 0)
    finish_first()
    finish_second()
    for g in ag_groups:
        for off in range(1, nz):
            spread_z(g, off).wait_send()
        spread_y(g, y_rows).wait_send()
        spread_core(g, core_rows).wait_send()


def per_device(
    n,
    kv_pool,
    block_table,
    lengths,
    queries,
    new_kv,
    residual_in,
    norm_gain,
    out_weight,
    gate_weight,
    up_weight,
    down_weight,
):
    steps = queries.shape[0]
    head_width = new_kv.shape[2] // 2
    head_count = queries.shape[2] // head_width
    heads_dev = head_count // n
    width = residual_in.shape[2]
    chunks = width // WIDE
    nz = n // 4
    positions = kv_pool.shape[0] * kv_pool.shape[1]

    q = queries.reshape(steps, -1)
    fresh = new_kv.reshape(steps, -1)
    residual = residual_in.reshape(steps, -1)
    gain = norm_gain.reshape(chunks, 8, 128)
    cache = kv_pool.reshape(positions, 2 * head_width)

    vmem = pl.BlockSpec(memory_space=pltpu.VMEM)
    smem = pl.BlockSpec(memory_space=pltpu.SMEM)
    hbm = pl.BlockSpec(memory_space=pl.ANY)
    dma = pltpu.SemaphoreType.DMA
    out = pl.pallas_call(
        functools.partial(layer_kernel, n),
        out_shape=jax.ShapeDtypeStruct((chunks, 16, 128), F32),
        in_specs=[smem, smem, vmem, vmem, vmem, vmem] + [hbm] * 5,
        out_specs=vmem,
        scratch_shapes=[
            pltpu.VMEM((positions, 2 * head_width), BF16),
            pltpu.VMEM(out_weight.shape, BF16),
            pltpu.VMEM(gate_weight.shape[::-1], BF16),
            pltpu.VMEM(up_weight.shape[::-1], BF16),
            pltpu.VMEM(down_weight.shape, BF16),
            pltpu.VMEM((n * 16, 128), F32),
            pltpu.VMEM((n, 16, 128), BF16),
            pltpu.VMEM((n, 16, 128), BF16),
            pltpu.VMEM((n * 16, 128), F32),
            pltpu.VMEM((2 * n, heads_dev * head_width), BF16),
            pltpu.VMEM((chunks, n * 16, 128), F32),
            pltpu.VMEM((2, chunks, n * 8, 128), BF16),
            pltpu.VMEM((2, chunks, n * 8, 128), BF16),
            pltpu.VMEM((chunks, n * 8, 128), F32),
            pltpu.VMEM((2, chunks, n * 4, 128), BF16),
            pltpu.VMEM((2, chunks, n * 4, 128), BF16),
            pltpu.VMEM((chunks, nz, 16, 128), F32),
            pltpu.VMEM((2, nz, chunks, 16, 128), BF16),
            pltpu.VMEM((2, nz, chunks, 16, 128), BF16),
            pltpu.VMEM((chunks, 16, 128), F32),
            pltpu.VMEM((chunks, n * 16, 128), BF16),
            pltpu.VMEM((n * 16, 128), F32),
            pltpu.VMEM((2 * n, WIDE), BF16),
            pltpu.VMEM((head_count * steps, head_width), F32),
            pltpu.VMEM((chunks, 16, 128), F32),
            pltpu.VMEM((16, 2 * head_width), F32),
            dma((2,)),
            dma((4, chunks)),
            dma((n,)),
            dma((n,)),
            dma((2, chunks)),
            dma((2, chunks)),
            dma((2, chunks)),
            dma((2, chunks)),
            dma((2, chunks, nz)),
            dma((2, chunks, nz)),
            dma((chunks, nz)),
            dma((chunks, nz)),
            dma((chunks,)),
            dma((chunks,)),
            dma((chunks,)),
            dma((chunks,)),
        ],
        compiler_params=pltpu.CompilerParams(
            collective_id=0, has_side_effects=True, vmem_limit_bytes=60 * 1024 * 1024
        ),
        cost_estimate=pl.CostEstimate(
            flops=2 * 2 * n * (out_weight.size + 3 * gate_weight.size),
            bytes_accessed=2 * (out_weight.size + 3 * gate_weight.size + cache.size),
            transcendentals=0,
        ),
        name="decode_layer",
    )(
        block_table,
        lengths,
        q,
        fresh,
        residual,
        gain,
        cache,
        out_weight,
        gate_weight.T,
        up_weight.T,
        down_weight,
    )
    return (
        out.reshape(chunks, steps, 8, 128).transpose(1, 0, 2, 3).reshape(steps, 1, width)
    )


def solution(mesh):
    placed = (
        P(("grp", "dev"), None, None),
        P(("grp", "dev"), None),
        P(("grp", "dev")),
        P(None, ("grp", "dev"), None),
        P(None, ("grp", "dev"), None),
        P(None, ("grp", "dev"), None),
        P(),
        P("dev", None),
        P(None, "dev"),
        P(None, "dev"),
        P("dev", None),
    )
    return jax.shard_map(
        functools.partial(per_device, mesh.shape["dev"]),
        mesh=mesh,
        in_specs=placed,
        out_specs=P(None, ("grp", "dev"), None),
        check_vma=False,
    )
```
